128 devices in a mesh: dp: 4 (over z), row: 4 (over y_lo, core), col: 8 (over x, y_hi).
Axes of the slice: x: 4, y: 4 (y_hi: 2, y_lo: 2; y = y_hi * 2 + y_lo), z: 4, core: 2. Of those that a mesh axis runs over, the one named last changes fastest.
Arguments:
- features: bfloat16 [4, 96, 768, 1024], P('dp', None, 'row', 'col'), may hold values from -6 to 6
- kernel: bfloat16 [8, 96, 3, 3], replicated, may hold values from -0.21875 to 0.21875
- target_amp: float32 [4, 8, 1024, 768], P('dp', None, ('row', 'col')), may hold values from 0.2 to 3
- spec_weight: float32 [8, 1024, 768], P(None, ('row', 'col')), may hold values from 0.1 to 10
Outputs:
- kernel_grad: float32 [8, 96, 3, 3], replicated
- feature_grad: bfloat16 [4, 96, 768, 1024], P('dp', None, 'row', 'col')
The draws below stay inside these ranges and needn't reach their ends.
All inputs are finite; a program needn't handle non-finite values.
Results may differ from the reference program's by a relative error of at most 0.015.
Values may be sent and summed in bfloat16 or wider, within the bound.
A program may use at most 256 MiB of HBM per device.

```python
import math
import jax
import jax.numpy as jnp
from jax import lax

C = 96
V = 8
B = 4
NX = 768
NY = 1024


def levels(key, shape, pieces, low, largest):
    def one(dim, blocks):
        heights = jax.random.uniform(jax.random.fold_in(jax.random.fold_in(key, 6), dim), (blocks,), jnp.float32, low / len(pieces), largest / len(pieces))
        return jnp.repeat(jnp.exp(heights), shape[dim] // blocks).reshape((-1,) + (1,) * (len(shape) - dim - 1))

    level = one(*pieces[0])
    for cut in pieces[1:]:
        level = level * one(*cut)
    return level


def bell_draw(rng, dims, scale, most, pieces=(), kind=jnp.bfloat16):
    result = jax.random.normal(rng, dims, jnp.float32) * scale
    if len(pieces) > 0:
        result = levels(rng, dims, pieces, -0.22, 0.18) * result
    return jnp.clip(result, min=-most, max=most).astype(kind)


def setup_inputs(seed: int = 0) -> dict:
    streams_of = jax.random.split(jax.random.key(seed), 5)
    features = bell_draw(streams_of[0], (B, C, NX, NY), 1.0, 6.0, ((0, 4), (2, 4), (3, 8)))
    kernel = bell_draw(streams_of[1], (V, C, 3, 3), (9 * C) ** -0.5, 0.21875)
    target_amp = jnp.clip(0.2 + 2.8 * jax.random.uniform(streams_of[2], (B, V, NY, NX), jnp.float32) ** levels(streams_of[2], (B, V, NY, NX), ((0, 4), (2, 32)), -0.2, 0.2), 0.2, 3.0)
    spec_weight = jnp.clip(jnp.exp(math.log(10.0) - 4.6051702 * jax.random.uniform(streams_of[3], (V, NY, NX), jnp.float32) ** levels(streams_of[3], (V, NY, NX), ((1, 32),), -0.2, 0.2)), 0.1, 10.0)
    return {"features": features, "kernel": kernel, "target_amp": target_amp, "spec_weight": spec_weight}


def convolve(field, weights):
    out = lax.conv_general_dilated(field[None], weights, (1, 1), ((1, 1), (1, 1)), dimension_numbers=('NCHW', 'OIHW', 'NCHW'), precision=lax.Precision.HIGHEST)
    return out[0]

def dft_tables(length):
    index = jnp.arange(length, dtype=jnp.int32)
    product = index[:, None] * index[None, :] % length
    angles = product.astype(jnp.float32) * (2.0 * math.pi / length)
    factor = 1.0 / math.sqrt(length)
    cos_half = (jnp.cos(angles) * factor).astype(jnp.bfloat16)
    sin_half = (jnp.sin(angles) * factor).astype(jnp.bfloat16)
    return (cos_half.astype(jnp.float32), sin_half.astype(jnp.float32))

def reference(features, kernel, target_amp, spec_weight):
    kernel_full = kernel.astype(jnp.float32)
    highest = lax.Precision.HIGHEST
    cos_y, sin_y = dft_tables(NY)
    cos_x, sin_x = dft_tables(NX)

    def one_sample(items):
        feature_map, target_one = items
        feature_full = feature_map.astype(jnp.float32)
        pred, pullback = jax.vjp(lambda weights, field: convolve(field, weights), kernel_full, feature_full)
        pred_half = pred.astype(jnp.bfloat16).astype(jnp.float32)
        half_re = jnp.einsum('vxy,ky->vxk', pred_half, cos_y, precision=highest).astype(jnp.bfloat16).astype(jnp.float32)
        half_im = (-jnp.einsum('vxy,ky->vxk', pred_half, sin_y, precision=highest)).astype(jnp.bfloat16).astype(jnp.float32)
        spec_re = jnp.einsum('kx,vxq->vqk', cos_x, half_re, precision=highest) + jnp.einsum('kx,vxq->vqk', sin_x, half_im, precision=highest)
        spec_im = jnp.einsum('kx,vxq->vqk', cos_x, half_im, precision=highest) - jnp.einsum('kx,vxq->vqk', sin_x, half_re, precision=highest)
        amp = jnp.sqrt(spec_re * spec_re + spec_im * spec_im + 1.0)
        factor = 2.0 * spec_weight * (amp - target_one) / amp
        grad_re = (factor * spec_re).astype(jnp.bfloat16).astype(jnp.float32)
        grad_im = (factor * spec_im).astype(jnp.bfloat16).astype(jnp.float32)
        back_re = (jnp.einsum('kx,vqk->vxq', cos_x, grad_re, precision=highest) - jnp.einsum('kx,vqk->vxq', sin_x, grad_im, precision=highest)).astype(jnp.bfloat16).astype(jnp.float32)
        back_im = (jnp.einsum('kx,vqk->vxq', sin_x, grad_re, precision=highest) + jnp.einsum('kx,vqk->vxq', cos_x, grad_im, precision=highest)).astype(jnp.bfloat16).astype(jnp.float32)
        dpred = jnp.einsum('vxk,ky->vxy', back_re, cos_y, precision=highest) - jnp.einsum('vxk,ky->vxy', back_im, sin_y, precision=highest)
        dpred_half = dpred.astype(jnp.bfloat16)
        kernel_part, feature_part = pullback(dpred_half.astype(pred.dtype))
        return (kernel_part, feature_part.astype(jnp.bfloat16))
    kernel_parts, feature_grad = lax.map(one_sample, (features, target_amp))
    kernel_grad = lax.optimization_barrier(jnp.sum(kernel_parts, axis=0)) / (B * NX * NY)
    return (kernel_grad, feature_grad)
```

```python
import math

import jax
import jax.numpy as jnp
import ml_dtypes
import numpy as np
from jax import lax
from jax.experimental import pallas as pl
from jax.experimental.pallas import tpu as pltpu
from jax.sharding import PartitionSpec as P

MESH = pl.DeviceIdType.MESH
F32 = jnp.float32
BF16 = jnp.bfloat16
VMEM_LIMIT = 56 * 1024 * 1024

C = 96
V = 8
NX = 768
NY = 1024
NDP = 4
NROW = 4
NCOL = 8
XB = NX // NROW
YB = NY // NCOL
QB = NY // (NROW * NCOL)
GROUP = 16
GROUPS = XB // GROUP
PACK = 2 * XB


def dft_tables(length):
    index = np.arange(length, dtype=np.int64)
    product = (index[:, None] * index[None, :]) % length
    angles = product * (2.0 * math.pi / length)
    factor = 1.0 / math.sqrt(length)
    return np.cos(angles) * factor, np.sin(angles) * factor


def spectral_tables():
    cos_y, sin_y = dft_tables(NY)
    along_y = np.concatenate([cos_y, -sin_y], axis=0)
    rim = np.zeros((2 * NY, 16 * NCOL))
    for k in range(NCOL):
        if k > 0:
            rim[:, 16 * k] = along_y[:, YB * k - 1]
        if k < NCOL - 1:
            rim[:, 16 * k + 1] = along_y[:, YB * (k + 1)]
    cos_x, sin_x = dft_tables(NX)
    from_re = np.concatenate([cos_x, -sin_x], axis=0).T.reshape(NX // 64, 64, 2 * NX)
    from_im = np.concatenate([sin_x, cos_x], axis=0).T.reshape(NX // 64, 64, 2 * NX)
    along_x = np.stack([from_re, from_im], axis=1).reshape(2 * NX, 2 * NX)
    bf16 = ml_dtypes.bfloat16
    return along_y.astype(bf16), rim.astype(bf16), along_x.astype(bf16)


def mm(a, b):
    return lax.dot_general(a, b, (((1,), (0,)), ((), ())), preferred_element_type=F32)


def mm_nt(a, b):
    return lax.dot_general(a, b, (((1,), (1,)), ((), ())), preferred_element_type=F32)


def lanes(shape):
    return lax.broadcasted_iota(jnp.int32, shape, len(shape) - 1)


def pick(row_lane_pairs, rows=16, width=128):
    r = lax.broadcasted_iota(jnp.int32, (rows, width), 0)
    c = lax.broadcasted_iota(jnp.int32, (rows, width), 1)
    hit = jnp.zeros((rows, width), F32)
    for row, lane in row_lane_pairs:
        hit = jnp.where((r == row) & (c == lane), 1.0, hit)
    return hit.astype(BF16)


def conv_kernel(feat, w, ft, pred, halo, turn, taps, whole, rim, send, recv):
    step = pl.program_id(0)
    row = lax.axis_index("row")
    up = lax.rem(row + NROW - 1, NROW)
    down = lax.rem(row + 1, NROW)
    group = jnp.where(step == 0, 0, jnp.where(step == 1, GROUPS - 1, step - 1))

    to_down = pltpu.make_async_remote_copy(
        src_ref=taps.at[XB, 0:24], dst_ref=taps.at[0, 0:24],
        send_sem=send.at[0], recv_sem=recv.at[0], device_id={"row": down}, device_id_type=MESH)
    to_up = pltpu.make_async_remote_copy(
        src_ref=taps.at[1, 48:72], dst_ref=taps.at[XB + 1, 48:72],
        send_sem=send.at[1], recv_sem=recv.at[1], device_id={"row": up}, device_id_type=MESH)

    @pl.when(step == 0)
    def _():
        barrier = pltpu.get_barrier_semaphore()
        pl.semaphore_signal(barrier, inc=1, device_id={"row": up}, device_id_type=MESH)
        pl.semaphore_signal(barrier, inc=1, device_id={"row": down}, device_id_type=MESH)
        pl.semaphore_wait(barrier, 2)

    turn[...] = feat[...].astype(F32).reshape(C * GROUP, YB)
    for x in range(GROUP):
        ft[x] = turn[pl.ds(x, C, stride=GROUP), :].astype(BF16)
    for pair in range(GROUP // 2):
        both = jnp.concatenate([ft[2 * pair], ft[2 * pair + 1]], axis=1)
        got = mm(w[...], both)
        taps[1 + GROUP * group + 2 * pair] = got[0:72, 0:YB]
        taps[2 + GROUP * group + 2 * pair] = got[0:72, YB : 2 * YB]

    @pl.when(step == 1)
    def _():
        to_down.start()
        to_up.start()

    @pl.when(step == GROUPS - 1)
    def _():
        to_down.wait()
        to_up.wait()

        @pl.when(row == 0)
        def _():
            taps[0, 0:24] = jnp.zeros((24, YB), F32)

        @pl.when(row == NROW - 1)
        def _():
            taps[XB + 1, 48:72] = jnp.zeros((24, YB), F32)

        lane = lanes((V * GROUP, YB))

        def combine(g, carry):
            x = GROUP * g
            total = (taps[pl.ds(x, GROUP), 0:24] + taps[pl.ds(x + 1, GROUP), 24:48]
                     + taps[pl.ds(x + 2, GROUP), 48:72])
            left = total[:, 0:8].reshape(V * GROUP, YB)
            mid = total[:, 8:16].reshape(V * GROUP, YB)
            right = total[:, 16:24].reshape(V * GROUP, YB)
            left = pltpu.roll(left, 1, 1)
            right = pltpu.roll(right, YB - 1, 1)
            at = pl.ds(pl.multiple_of(V * GROUP * g, V * GROUP), V * GROUP)
            whole[at, :] = mid + jnp.where(lane == 0, 0.0, left) + jnp.where(lane == YB - 1, 0.0, right)
            rim[at, :] = jnp.where(lane == 0, left, right)
            return carry

        lax.fori_loop(0, GROUPS, combine, 0)
        chosen = pick([(0, YB - 1), (1, 0)])
        for v in range(V):
            pred[v] = whole[pl.ds(v, XB, stride=V), :].astype(BF16)
            edge = mm_nt(chosen, rim[pl.ds(v, XB, stride=V), :].astype(BF16))
            halo[v] = jnp.concatenate([edge, jnp.zeros((16, 256 - XB), F32)], axis=1).astype(BF16)


def convolve(features, weights):
    def place(i):
        return jnp.where(i == 0, 0, jnp.where(i == 1, GROUPS - 1, i - 1))

    return pl.pallas_call(
        conv_kernel,
        grid=(GROUPS,),
        in_specs=[
            pl.BlockSpec((C, GROUP, YB), lambda i: (0, place(i), 0)),
            pl.BlockSpec((80, C), lambda i: (0, 0)),
        ],
        out_specs=[
            pl.BlockSpec((GROUP, C, YB), lambda i: (place(i), 0, 0)),
            pl.BlockSpec((V, XB, YB), lambda i: (0, 0, 0)),
            pl.BlockSpec((V, 16, 256), lambda i: (0, 0, 0)),
        ],
        out_shape=[
            jax.ShapeDtypeStruct((XB, C, YB), BF16),
            jax.ShapeDtypeStruct((V, XB, YB), BF16),
            jax.ShapeDtypeStruct((V, 16, 256), BF16),
        ],
        scratch_shapes=[
            pltpu.VMEM((C * GROUP, YB), F32),
            pltpu.VMEM((XB + 2, 72, YB), F32),
            pltpu.VMEM((XB * V, YB), F32),
            pltpu.VMEM((XB * V, YB), F32),
            pltpu.SemaphoreType.DMA((2,)),
            pltpu.SemaphoreType.DMA((2,)),
        ],
        compiler_params=pltpu.CompilerParams(
            collective_id=0, has_side_effects=True, vmem_limit_bytes=VMEM_LIMIT),
        name="convolve",
    )(features, weights)


def spectral_kernel(pred, halo, t1_hbm, rim_hbm, t2_hbm, targ_hbm, wt_hbm, tiles, rims,
                    t1, t1rim, t2, targ, wt, lines, rim_in, half, spec, grads, back, coef, flat,
                    dp_out, rim_out,
                    load, s1, r1, s1h, r1h, s2, r2, s3, r3, s4, r4, s4h, r4h):
    row = lax.axis_index("row")
    col = lax.axis_index("col")
    me = NCOL * row + col
    everyone = NROW * NCOL

    loads = [pltpu.make_async_copy(src, dst, load.at[n]) for n, (src, dst) in enumerate(
        [(t1_hbm, t1), (rim_hbm, t1rim), (t2_hbm, t2), (targ_hbm, targ), (wt_hbm, wt)])]
    for one in loads:
        one.start()

    barrier = pltpu.get_barrier_semaphore()

    def greet(d, carry):
        other = lax.rem(me + d, everyone)
        pl.semaphore_signal(barrier, inc=1, device_id={"row": other // NCOL, "col": lax.rem(other, NCOL)},
                            device_id_type=MESH)
        return carry

    lax.fori_loop(1, everyone, greet, 0)
    pl.semaphore_wait(barrier, everyone - 1)

    def line_copy(k, source):
        return pltpu.make_async_remote_copy(
            src_ref=pred.at[k], dst_ref=lines.at[0:XB, pl.ds(pl.multiple_of(YB * source, YB), YB)],
            send_sem=s1.at[k], recv_sem=r1.at[source], device_id={"col": k}, device_id_type=MESH)

    def line_rim_copy(k, source):
        return pltpu.make_async_remote_copy(
            src_ref=halo.at[k], dst_ref=rim_in.at[pl.ds(pl.multiple_of(16 * source, 16), 16), :],
            send_sem=s1h.at[k], recv_sem=r1h.at[source], device_id={"col": k}, device_id_type=MESH)

    def send_lines(d, carry):
        k = lax.rem(col + d, NCOL)
        line_copy(k, col).start()
        line_rim_copy(k, col).start()
        return carry

    lax.fori_loop(1, NCOL, send_lines, 0)
    own_line = pltpu.make_async_copy(
        pred.at[col], lines.at[0:XB, pl.ds(pl.multiple_of(YB * col, YB), YB)], r1.at[col])
    own_rim = pltpu.make_async_copy(
        halo.at[col], rim_in.at[pl.ds(pl.multiple_of(16 * col, 16), 16), :], r1h.at[col])
    own_line.start()
    own_rim.start()
    lines[XB:256, :] = jnp.zeros((256 - XB, NY), BF16)
    loads[0].wait()
    loads[1].wait()
    own_line.wait()
    own_rim.wait()

    def wait_lines(d, carry):
        k = lax.rem(col + d, NCOL)
        line_copy(k, k).wait_recv()
        line_rim_copy(k, k).wait_recv()
        return carry

    lax.fori_loop(1, NCOL, wait_lines, 0)

    def half_copy(j, source):
        return pltpu.make_async_remote_copy(
            src_ref=half.at[pl.ds(pl.multiple_of(QB * j, QB), QB), :],
            dst_ref=spec.at[pl.ds(pl.multiple_of(QB * lax.rem(source, NCOL), QB), QB),
                            pl.ds(pl.multiple_of(PACK * (source // NCOL), PACK), PACK)],
            send_sem=s2.at[j], recv_sem=r2.at[source],
            device_id={"row": j // NCOL, "col": lax.rem(j, NCOL)}, device_id_type=MESH)

    own_half = pltpu.make_async_copy(
        half.at[pl.ds(pl.multiple_of(QB * me, QB), QB), :],
        spec.at[pl.ds(pl.multiple_of(QB * col, QB), QB), pl.ds(pl.multiple_of(PACK * row, PACK), PACK)],
        r2.at[me])
    first64 = lanes((128, 128)) < 64

    def along_y(c, carry):
        chunk = lax.rem(c + me // 4 + 1, 8)
        q = pl.multiple_of(128 * chunk, 128)
        re = mm_nt(t1[pl.ds(q, 128), :], lines[...]) + mm(t1rim[pl.ds(q, 128), :], rim_in[...])
        im = mm_nt(t1[pl.ds(NY + q, 128), :], lines[...]) + mm(t1rim[pl.ds(NY + q, 128), :], rim_in[...])
        re0, re1 = re[:, 0:128], re[:, 128:256]
        im0, im1 = im[:, 0:128], im[:, 128:256]
        half[pl.ds(q, 128), 0:128] = jnp.where(first64, re0, pltpu.roll(im0, 64, 1)).astype(BF16)
        half[pl.ds(q, 128), 128:256] = jnp.where(first64, pltpu.roll(re0, 64, 1), im0).astype(BF16)
        half[pl.ds(q, 128), 256:384] = jnp.where(first64, re1, pltpu.roll(im1, 64, 1)).astype(BF16)
        for m in range(4):
            j = 4 * chunk + m

            @pl.when(j != me)
            def _():
                half_copy(j, me).start()

            @pl.when(j == me)
            def _():
                own_half.start()

        return carry

    lax.fori_loop(0, 8, along_y, 0)
    loads[2].wait()
    loads[3].wait()
    loads[4].wait()
    own_half.wait()

    def wait_half(d, carry):
        other = lax.rem(me + d, everyone)
        half_copy(other, other).wait_recv()
        return carry

    lax.fori_loop(1, everyone, wait_half, 0)

    def along_x(c, carry):
        p = pl.ds(pl.multiple_of(256 * c, 256), 256)
        p_im = pl.ds(pl.multiple_of(NX + 256 * c, 256), 256)
        re = mm(spec[...], t2[:, p])
        im = mm(spec[...], t2[:, p_im])
        amp = jnp.sqrt(re * re + im * im + 1.0)
        factor = 2.0 * wt[:, p] * (amp - targ[:, p]) / amp
        grads[:, p] = (factor * re).astype(BF16)
        grads[:, p_im] = (factor * im).astype(BF16)
        return carry

    lax.fori_loop(0, 3, along_x, 0)

    def back_copy(r, v, source):
        return pltpu.make_async_remote_copy(
            src_ref=back.at[r, pl.ds(pl.multiple_of(QB * v, QB), QB), :],
            dst_ref=coef.at[pl.ds(pl.multiple_of(QB * source, QB), QB), :],
            send_sem=s3.at[NCOL * r + v], recv_sem=r3.at[source],
            device_id={"row": r, "col": v}, device_id_type=MESH)

    own_back = pltpu.make_async_copy(
        back.at[row, pl.ds(pl.multiple_of(QB * col, QB), QB), :],
        coef.at[pl.ds(pl.multiple_of(QB * me, QB), QB), :], r3.at[me])

    def back_x(c, carry):
        r = lax.rem(row + 1 + c, NROW)
        back[r] = mm_nt(grads[...], t2[pl.ds(pl.multiple_of(PACK * r, PACK), PACK), :]).astype(BF16)
        for d in range(NCOL):
            v = lax.rem(col + d, NCOL)
            if d > 0:
                back_copy(r, v, me).start()
            else:
                @pl.when(r != row)
                def _():
                    back_copy(r, v, me).start()

                @pl.when(r == row)
                def _():
                    own_back.start()

        return carry

    lax.fori_loop(0, NROW, back_x, 0)
    own_back.wait()

    def wait_back(d, carry):
        other = lax.rem(me + d, everyone)
        back_copy(other // NCOL, lax.rem(other, NCOL), other).wait_recv()
        return carry

    lax.fori_loop(1, everyone, wait_back, 0)

    for b in range(3):
        turned = coef[:, 128 * b : 128 * b + 128].T
        flat[64 * b : 64 * b + 64, 0:NY] = turned[0:64]
        flat[64 * b : 64 * b + 64, NY : 2 * NY] = turned[64:128]

    def tile_copy(k, source):
        return pltpu.make_async_remote_copy(
            src_ref=dp_out.at[k], dst_ref=tiles.at[source],
            send_sem=s4.at[k], recv_sem=r4.at[source], device_id={"col": k}, device_id_type=MESH)

    def tile_rim_copy(k, source):
        return pltpu.make_async_remote_copy(
            src_ref=rim_out.at[k], dst_ref=rims.at[pl.ds(pl.multiple_of(16 * source, 16), 16), :],
            send_sem=s4h.at[k], recv_sem=r4h.at[source], device_id={"col": k}, device_id_type=MESH)

    own_tile = pltpu.make_async_copy(dp_out.at[col], tiles.at[col], r4.at[col])
    own_tile_rim = pltpu.make_async_copy(
        rim_out.at[col], rims.at[pl.ds(pl.multiple_of(16 * col, 16), 16), :], r4h.at[col])

    def back_y(c, carry):
        block = lax.rem(c + col // 2 + 1, NCOL // 2)
        cells = mm(flat[...], t1[:, pl.ds(pl.multiple_of(256 * block, 256), 256)]).astype(BF16)
        for m in range(2):
            k = 2 * block + m
            dp_out[k] = cells[:, 128 * m : 128 * m + 128]

            @pl.when(k != col)
            def _():
                tile_copy(k, col).start()

            @pl.when(k == col)
            def _():
                own_tile.start()

        return carry

    lax.fori_loop(0, NCOL // 2, back_y, 0)
    before = pick([(0, YB - 1)])
    after = pick([(1, 0)])
    for k in range(NCOL):
        edge = jnp.zeros((16, XB), F32)
        if k > 0:
            edge = edge + mm_nt(before, dp_out[k - 1])
        if k < NCOL - 1:
            edge = edge + mm_nt(after, dp_out[k + 1])
        rim_out[k] = jnp.concatenate([edge, jnp.zeros((16, 256 - XB), F32)], axis=1).astype(BF16)

        @pl.when(k != col)
        def _():
            tile_rim_copy(k, col).start()

        @pl.when(k == col)
        def _():
            own_tile_rim.start()

    own_tile.wait()
    own_tile_rim.wait()

    def finish_col(d, carry):
        k = lax.rem(col + d, NCOL)
        tile_copy(k, k).wait_recv()
        tile_rim_copy(k, k).wait_recv()
        line_copy(k, col).wait_send()
        line_rim_copy(k, col).wait_send()
        tile_copy(k, col).wait_send()
        tile_rim_copy(k, col).wait_send()
        return carry

    lax.fori_loop(1, NCOL, finish_col, 0)

    def finish_all(d, carry):
        other = lax.rem(me + d, everyone)
        half_copy(other, me).wait_send()
        back_copy(other // NCOL, lax.rem(other, NCOL), me).wait_send()
        return carry

    lax.fori_loop(1, everyone, finish_all, 0)


def transform(pred, halo, target, weight):
    along_y, rim, along_x = spectral_tables()
    vmem = pl.BlockSpec(memory_space=pltpu.VMEM)
    anywhere = pl.BlockSpec(memory_space=pl.ANY)
    dma = pltpu.SemaphoreType.DMA
    everyone = NROW * NCOL
    return pl.pallas_call(
        spectral_kernel,
        in_specs=[vmem, vmem] + [anywhere] * 5,
        out_specs=[vmem, vmem],
        out_shape=[
            jax.ShapeDtypeStruct((V, XB, YB), BF16),
            jax.ShapeDtypeStruct((V * 16, 256), BF16),
        ],
        scratch_shapes=[
            pltpu.VMEM((2 * NY, NY), BF16),
            pltpu.VMEM((2 * NY, 16 * NCOL), BF16),
            pltpu.VMEM((2 * NX, 2 * NX), BF16),
            pltpu.VMEM((V * QB, NX), F32),
            pltpu.VMEM((V * QB, NX), F32),
            pltpu.VMEM((256, NY), BF16),
            pltpu.VMEM((16 * NCOL, 256), BF16),
            pltpu.VMEM((NY, PACK), BF16),
            pltpu.VMEM((V * QB, 2 * NX), BF16),
            pltpu.VMEM((V * QB, 2 * NX), BF16),
            pltpu.VMEM((NROW, V * QB, PACK), BF16),
            pltpu.VMEM((NY, PACK), BF16),
            pltpu.VMEM((XB, 2 * NY), BF16),
            pltpu.VMEM((NCOL, XB, YB), BF16),
            pltpu.VMEM((NCOL, 16, 256), BF16),
            dma((5,)),
            dma((NCOL,)), dma((NCOL,)), dma((NCOL,)), dma((NCOL,)),
            dma((everyone,)), dma((everyone,)), dma((everyone,)), dma((everyone,)),
            dma((NCOL,)), dma((NCOL,)), dma((NCOL,)), dma((NCOL,)),
        ],
        compiler_params=pltpu.CompilerParams(
            collective_id=1, has_side_effects=True, vmem_limit_bytes=VMEM_LIMIT),
        name="transform",
    )(pred, halo, jnp.asarray(along_y), jnp.asarray(rim), jnp.asarray(along_x), target, weight)


def kgrad_kernel(tiles, rims, ft, shifted, grad, wide, mine, got_dp, got_row, got_col,
                 send, recv, s_dp, r_dp, s_row, r_row, s_col, r_col):
    dp = lax.axis_index("dp")
    row = lax.axis_index("row")
    col = lax.axis_index("col")
    up = lax.rem(row + NROW - 1, NROW)
    down = lax.rem(row + 1, NROW)
    axes = (("dp", dp, NDP), ("row", row, NROW), ("col", col, NCOL))

    barrier = pltpu.get_barrier_semaphore()
    for name, at, count in axes:
        for d in range(1, count):
            pl.semaphore_signal(barrier, inc=1, device_id={name: lax.rem(at + d, count)}, device_id_type=MESH)
    pl.semaphore_wait(barrier, NDP + NROW + NCOL - 3)

    columns = rims[...].astype(F32).T.astype(BF16)
    lane = lanes((XB, YB))
    for v in range(V):
        cells = tiles[v].astype(F32)
        edge = mm(columns[0:XB], pick([(16 * v, 0), (16 * v + 1, YB - 1)], rows=128))
        wide[pl.ds(v, XB, stride=32), :] = jnp.where(lane == YB - 1, edge, pltpu.roll(cells, YB - 1, 1))
        wide[pl.ds(8 + v, XB, stride=32), :] = cells
        wide[pl.ds(16 + v, XB, stride=32), :] = jnp.where(lane == 0, edge, pltpu.roll(cells, 1, 1))
        wide[pl.ds(24 + v, XB, stride=32), :] = jnp.zeros((XB, YB), F32)

    def narrow(g, carry):
        at = pl.multiple_of(512 * g, 512)
        shifted[pl.ds(32 + at, 512), :] = wide[pl.ds(at, 512), :].astype(BF16)
        return carry

    lax.fori_loop(0, GROUPS, narrow, 0)
    to_down = pltpu.make_async_remote_copy(
        src_ref=shifted.at[32 * XB : 32 * XB + 32], dst_ref=shifted.at[0:32],
        send_sem=send.at[0], recv_sem=recv.at[0], device_id={"row": down}, device_id_type=MESH)
    to_up = pltpu.make_async_remote_copy(
        src_ref=shifted.at[32:64], dst_ref=shifted.at[32 * XB + 32 : 32 * XB + 64],
        send_sem=send.at[1], recv_sem=recv.at[1], device_id={"row": up}, device_id_type=MESH)
    to_down.start()
    to_up.start()

    def gather(g, total):
        for pair in range(GROUP // 2):
            x = GROUP * g + 2 * pair
            at = pl.multiple_of(32 * x, 32)
            rows = jnp.concatenate([shifted[pl.ds(at, 96), :], shifted[pl.ds(at + 32, 96), :]], axis=1)
            cells = jnp.concatenate([ft[x], ft[x + 1]], axis=1)
            total = total + mm_nt(rows, cells)
        return total

    total = lax.fori_loop(1, GROUPS - 1, gather, jnp.zeros((96, C), F32))
    to_down.wait()
    to_up.wait()

    @pl.when(row == 0)
    def _():
        shifted[0:32] = jnp.zeros((32, YB), BF16)

    @pl.when(row == NROW - 1)
    def _():
        shifted[32 * XB + 32 : 32 * XB + 64] = jnp.zeros((32, YB), BF16)

    total = gather(0, total)
    total = gather(GROUPS - 1, total)
    total = jnp.concatenate([total, jnp.zeros((96, 128 - C), F32)], axis=1)
    mine[0] = jnp.concatenate([total[0:24], total[32:56], total[64:88]], axis=0)

    stages = ((axes[0], got_dp, s_dp, r_dp), (axes[1], got_row, s_row, r_row), (axes[2], got_col, s_col, r_col))
    for stage, ((name, at, count), got, s_sem, r_sem) in enumerate(stages):
        copies = [
            pltpu.make_async_remote_copy(
                src_ref=mine.at[stage], dst_ref=got.at[d - 1], send_sem=s_sem.at[d - 1], recv_sem=r_sem.at[d - 1],
                device_id={name: lax.rem(at + d, count)}, device_id_type=MESH)
            for d in range(1, count)
        ]
        for one in copies:
            one.start()
        total = mine[stage]
        for d in range(1, count):
            copies[d - 1].wait_recv()
        for source in range(count):
            term = mine[stage]
            for d in range(1, count):
                term = jnp.where(lax.rem(source + d, count) == at, got[d - 1], term)
            total = term if source == 0 else total + term
        if stage < 2:
            mine[stage + 1] = total
        else:
            grad[...] = total
        for one in copies:
            one.wait_send()


def kernel_gradient(tiles, rims, ft):
    vmem = pl.BlockSpec(memory_space=pltpu.VMEM)
    dma = pltpu.SemaphoreType.DMA
    return pl.pallas_call(
        kgrad_kernel,
        in_specs=[vmem] * 3,
        out_specs=[vmem] * 2,
        out_shape=[
            jax.ShapeDtypeStruct((32 * (XB + 2), YB), BF16),
            jax.ShapeDtypeStruct((72, 128), F32),
        ],
        scratch_shapes=[
            pltpu.VMEM((32 * XB, YB), F32),
            pltpu.VMEM((3, 72, 128), F32),
            pltpu.VMEM((NDP - 1, 72, 128), F32),
            pltpu.VMEM((NROW - 1, 72, 128), F32),
            pltpu.VMEM((NCOL - 1, 72, 128), F32),
            dma((2,)), dma((2,)),
            dma((NDP - 1,)), dma((NDP - 1,)),
            dma((NROW - 1,)), dma((NROW - 1,)),
            dma((NCOL - 1,)), dma((NCOL - 1,)),
        ],
        compiler_params=pltpu.CompilerParams(
            collective_id=2, has_side_effects=True, vmem_limit_bytes=VMEM_LIMIT),
        name="kernel_gradient",
    )(tiles, rims, ft)


def fgrad_kernel(shifted, w, out, turn):
    group = pl.program_id(0)
    for pair in range(GROUP // 2):
        at = pl.multiple_of(32 * (GROUP * group + 2 * pair), 32)
        rows = jnp.concatenate([shifted[pl.ds(at, 96), :], shifted[pl.ds(at + 32, 96), :]], axis=1)
        got = mm(w[...], rows)
        turn[pl.ds(2 * pair, C, stride=GROUP), :] = got[:, 0:YB]
        turn[pl.ds(2 * pair + 1, C, stride=GROUP), :] = got[:, YB : 2 * YB]
    out[...] = turn[...].reshape(C, GROUP, YB).astype(BF16)


def feature_gradient(shifted, weights):
    return pl.pallas_call(
        fgrad_kernel,
        grid=(GROUPS,),
        in_specs=[
            pl.BlockSpec((32 * (XB + 2), YB), lambda i: (0, 0)),
            pl.BlockSpec((C, 96), lambda i: (0, 0)),
        ],
        out_specs=pl.BlockSpec((C, GROUP, YB), lambda i: (0, i, 0)),
        out_shape=jax.ShapeDtypeStruct((C, XB, YB), BF16),
        scratch_shapes=[pltpu.VMEM((C * GROUP, YB), F32)],
        compiler_params=pltpu.CompilerParams(vmem_limit_bytes=VMEM_LIMIT),
        name="feature_gradient",
    )(shifted, weights)


def per_device(features, kernel, target_amp, spec_weight):
    by_tap = kernel.transpose(2, 3, 0, 1)
    w_forward = jnp.pad(by_tap.reshape(72, C), ((0, 8), (0, 0)))
    w_back = jnp.pad(by_tap[::-1], ((0, 0), (0, 1), (0, 0), (0, 0))).reshape(96, C).T
    ft, pred, halo = convolve(features.reshape(C, XB, YB), w_forward)
    tiles, rims = transform(pred, halo, target_amp.reshape(V * QB, NX), spec_weight.reshape(V * QB, NX))
    shifted, grad = kernel_gradient(tiles, rims, ft)
    feature_grad = feature_gradient(shifted, w_back).reshape(1, C, XB, YB)
    grad = grad[:, 0:C].reshape(3, 3, V, C)[::-1].transpose(2, 3, 0, 1)
    cells = NDP * NX * NY
    return grad / cells, feature_grad


def solution(mesh):
    return jax.shard_map(
        per_device,
        mesh=mesh,
        in_specs=(
            P("dp", None, "row", "col"),
            P(),
            P("dp", None, ("row", "col"), None),
            P(None, ("row", "col"), None),
        ),
        out_specs=(P(), P("dp", None, "row", "col")),
        check_vma=False,
    )
```

```python
import math

import jax
import jax.numpy as jnp
import ml_dtypes
import numpy as np
from jax import lax
from jax.experimental import pallas as pl
from jax.experimental.pallas import tpu as pltpu
from jax.sharding import PartitionSpec as P

MESH = pl.DeviceIdType.MESH
F32 = jnp.float32
BF16 = jnp.bfloat16
VMEM_LIMIT = 56 * 1024 * 1024

C = 96
V = 8
NX = 768
NY = 1024
NDP = 4
NROW = 4
NCOL = 8
XB = NX // NROW
YB = NY // NCOL
QB = NY // (NROW * NCOL)
HALF = NY // 2
GROUP = 16
GROUPS = XB // GROUP
PACK = 2 * XB


def dft_tables(length):
    index = np.arange(length, dtype=np.int64)
    product = (index[:, None] * index[None, :]) % length
    angles = product * (2.0 * math.pi / length)
    factor = 1.0 / math.sqrt(length)
    return np.cos(angles) * factor, np.sin(angles) * factor


def spectral_tables():
    cos_y, sin_y = dft_tables(NY)
    along_y = np.concatenate([cos_y[0:HALF], -sin_y[0:HALF]], axis=0)
    along_y[HALF] = cos_y[HALF]
    rim = np.zeros((NY, 16 * NCOL))
    for k in range(NCOL):
        if k > 0:
            rim[:, 16 * k] = along_y[:, YB * k - 1]
        if k < NCOL - 1:
            rim[:, 16 * k + 1] = along_y[:, YB * (k + 1)]
    cos_x, sin_x = dft_tables(NX)
    from_re = np.concatenate([cos_x, -sin_x], axis=0).T.reshape(NX // 64, 64, 2 * NX)
    from_im = np.concatenate([sin_x, cos_x], axis=0).T.reshape(NX // 64, 64, 2 * NX)
    along_x = np.stack([from_re, from_im], axis=1).reshape(2 * NX, 2 * NX)
    flip = np.zeros((NX, NX))
    flip[(NX - np.arange(NX)) % NX, np.arange(NX)] = 1.0
    bf16 = ml_dtypes.bfloat16
    return along_y.astype(bf16), rim.astype(bf16), along_x.astype(bf16), flip.astype(bf16)


def mm(a, b):
    return lax.dot_general(a, b, (((1,), (0,)), ((), ())), preferred_element_type=F32)


def mm_nt(a, b):
    return lax.dot_general(a, b, (((1,), (1,)), ((), ())), preferred_element_type=F32)


def lanes(shape):
    return lax.broadcasted_iota(jnp.int32, shape, len(shape) - 1)


def pick(row_lane_pairs, rows=16, width=128):
    r = lax.broadcasted_iota(jnp.int32, (rows, width), 0)
    c = lax.broadcasted_iota(jnp.int32, (rows, width), 1)
    hit = jnp.zeros((rows, width), F32)
    for row, lane in row_lane_pairs:
        hit = jnp.where((r == row) & (c == lane), 1.0, hit)
    return hit.astype(BF16)


def main_kernel(feat_hbm, w, t1_hbm, rim_hbm, t2_hbm, flip_hbm, targ_hbm, wt_hbm,
                shifted, grad,
                feat, ft, taps, pred, edges, halo, t1, t1rim, t2, flip, targ, wt,
                own_a, own_b, got_a, got_b, rows_out, rows_in, map_a, map_b,
                lines, rim_in, half, spec, grads, back, coef, flat, dp_out, rim_out, tiles, rims, columns,
                part, slots, mine, slots_col, total_ref,
                lf, load, sx, rx, sp, rp, s1, r1, s1h, r1h, s2, r2, s3, r3, s4, r4, s4h, r4h, sy, ry,
                sa, ra, sb, rb, sc, rc):
    dp = lax.axis_index("dp")
    row = lax.axis_index("row")
    col = lax.axis_index("col")
    me = NCOL * row + col
    up = lax.rem(row + NROW - 1, NROW)
    down = lax.rem(row + 1, NROW)
    low = me < 16
    block = jnp.where(low, me, 31 - me)
    vhalf = lax.rem(row, 2)
    group16 = NROW * dp + row

    def remote(src, dst, send, recv, where):
        return pltpu.make_async_remote_copy(
            src_ref=src, dst_ref=dst, send_sem=send, recv_sem=recv, device_id=where, device_id_type=MESH)

    def plane(j):
        return {"row": j // NCOL, "col": lax.rem(j, NCOL)}

    def rows(start, size):
        return pl.ds(pl.multiple_of(start, size), size)

    def feat_copy(g):
        at = rows(GROUP * g, GROUP)
        return pltpu.make_async_copy(feat_hbm.at[:, at], feat.at[:, at], lf.at[g])

    for i in range(GROUPS):
        feat_copy((i + GROUPS - 1) % GROUPS).start()
    loads = [pltpu.make_async_copy(src, dst, load.at[n]) for n, (src, dst) in enumerate(
        [(targ_hbm, targ), (wt_hbm, wt), (t1_hbm, t1), (rim_hbm, t1rim), (flip_hbm, flip), (t2_hbm, t2)])]
    loads[0].start()
    loads[1].start()

    barrier = pltpu.get_barrier_semaphore()

    def greet(d, carry):
        pl.semaphore_signal(barrier, inc=1, device_id=plane(lax.rem(me + d, 32)), device_id_type=MESH)
        return carry

    lax.fori_loop(1, 32, greet, 0)
    for d in range(1, NDP):
        for r in range(NROW):
            pl.semaphore_signal(barrier, inc=1, device_id={"dp": lax.rem(dp + d, NDP), "row": r}, device_id_type=MESH)

    def conv_group(i, carry):
        g = lax.rem(i + GROUPS - 1, GROUPS)
        feat_copy(g).wait()
        at = rows(GROUP * g, GROUP)
        ft[at] = jnp.swapaxes(feat[:, at, :], 0, 1)
        for pair in range(GROUP // 2):
            x = GROUP * g + 2 * pair
            got = mm(w[...], jnp.concatenate([ft[x], ft[x + 1]], axis=1))
            taps[1 + x] = got[0:72, 0:YB]
            taps[2 + x] = got[0:72, YB : 2 * YB]
        return carry

    lax.fori_loop(0, 3, conv_group, 0)
    pl.semaphore_wait(barrier, 31 + 12)
    to_down = remote(taps.at[XB, 0:24], taps.at[0, 0:24], sx.at[0], rx.at[0], {"row": down})
    to_up = remote(taps.at[1, 48:72], taps.at[XB + 1, 48:72], sx.at[1], rx.at[1], {"row": up})
    to_down.start()
    to_up.start()

    loads[0].wait()
    loads[1].wait()
    for one in loads[2:]:
        one.start()
    own_a[...] = (2.0 * wt[...]).astype(BF16)
    own_b[...] = (2.0 * wt[...] * targ[...]).astype(BF16)
    rows_out[...] = jnp.zeros((2, 16, NX), F32)
    for v in range(V):
        first = 2.0 * wt[QB * v : QB * v + 1, :]
        rows_out[v // 4, v % 4 : v % 4 + 1, :] = first
        rows_out[v // 4, 8 + v % 4 : 9 + v % 4, :] = first * targ[QB * v : QB * v + 1, :]
    partner = {"row": NROW - 1 - row, "col": NCOL - 1 - col}
    theirs = rows(128 * (1 - vhalf), 128)
    swap_a = remote(own_a.at[theirs], got_a, sp.at[0], rp.at[0], partner)
    swap_b = remote(own_b.at[theirs], got_b, sp.at[1], rp.at[1], partner)
    swap_a.start()
    swap_b.start()
    first_of = lax.rem(32 - me, 16)
    first_of = jnp.where(low, 0, first_of)
    row_low = remote(rows_out.at[first_of // 8], rows_in, sp.at[2], rp.at[2], plane(first_of))
    row_high = remote(rows_out.at[1 - first_of // 8], rows_in, sp.at[3], rp.at[2], plane(31 - first_of))

    @pl.when(me >= 16)
    def _():
        row_low.start()
        row_high.start()

    def line_copy(b, k, source):
        return remote(pred.at[k, 64 * b : 64 * b + 64],
                      lines.at[64 * b : 64 * b + 64, rows(YB * source, YB)],
                      s1.at[b, k], r1.at[b, source], {"col": k})

    def line_rim_copy(k, source):
        return remote(halo.at[k], rim_in.at[rows(16 * source, 16), :], s1h.at[k], r1h.at[source], {"col": k})

    def own_line(b):
        return pltpu.make_async_copy(pred.at[col, 64 * b : 64 * b + 64],
                                     lines.at[64 * b : 64 * b + 64, rows(YB * col, YB)], r1.at[b, col])

    own_rim = pltpu.make_async_copy(halo.at[col], rim_in.at[rows(16 * col, 16), :], r1h.at[col])
    lane128 = lanes((V * GROUP, YB))

    def combine(g, carry):
        x = GROUP * g
        total = (taps[pl.ds(x, GROUP), 0:24] + taps[pl.ds(x + 1, GROUP), 24:48]
                 + taps[pl.ds(x + 2, GROUP), 48:72])
        left = pltpu.roll(total[:, 0:8].reshape(V * GROUP, YB), 1, 1)
        mid = total[:, 8:16].reshape(V * GROUP, YB)
        right = pltpu.roll(total[:, 16:24].reshape(V * GROUP, YB), YB - 1, 1)
        cells = mid + jnp.where(lane128 == 0, 0.0, left) + jnp.where(lane128 == YB - 1, 0.0, right)
        edge = jnp.where(lane128 == 0, left, right)
        at = rows(x, GROUP)
        pred[:, at, :] = jnp.swapaxes(cells.reshape(GROUP, V, YB), 0, 1).astype(BF16)
        edges[:, at, :] = jnp.swapaxes(edge.reshape(GROUP, V, YB), 0, 1).astype(BF16)
        return carry

    def send_lines(b):
        def one(d, carry):
            line_copy(b, lax.rem(col + d, NCOL), col).start()
            return carry

        lax.fori_loop(1, NCOL, one, 0)
        own_line(b).start()

    lax.fori_loop(3, 6, conv_group, 0)
    to_down.wait()
    to_up.wait()

    @pl.when(row == 0)
    def _():
        taps[0, 0:24] = jnp.zeros((24, YB), F32)

    @pl.when(row == NROW - 1)
    def _():
        taps[XB + 1, 48:72] = jnp.zeros((24, YB), F32)

    lax.fori_loop(0, 4, combine, 0)
    send_lines(0)
    lax.fori_loop(6, 10, conv_group, 0)
    lax.fori_loop(4, 8, combine, 0)
    send_lines(1)
    lax.fori_loop(10, 12, conv_group, 0)
    lax.fori_loop(8, 12, combine, 0)
    send_lines(2)
    chosen = pick([(0, YB - 1), (1, 0)])
    for v in range(V):
        edge = mm_nt(chosen, edges[v])
        halo[v] = jnp.concatenate([edge, jnp.zeros((16, 256 - XB), F32)], axis=1).astype(BF16)

    def send_rims(d, carry):
        line_rim_copy(lax.rem(col + d, NCOL), col).start()
        return carry

    lax.fori_loop(1, NCOL, send_rims, 0)
    own_rim.start()

    for one in loads[2:]:
        one.wait()
    swap_a.wait_recv()
    swap_b.wait_recv()
    row_low.wait_recv()
    ours = rows(128 * vhalf, 128)
    r2d = lax.broadcasted_iota(jnp.int32, (128, 128), 0)
    c2d = lax.broadcasted_iota(jnp.int32, (128, 128), 1)
    mirror = jnp.where((r2d // QB == c2d // QB) & (lax.rem(r2d, QB) + lax.rem(c2d, QB) == QB), 1.0, 0.0).astype(BF16)
    sub16 = lax.broadcasted_iota(jnp.int32, (16, NX), 0)
    at_zero = jnp.where(block == 0, 1.0, 0.0)
    firsts = rows_in[...]
    firsts_half = (firsts * (1.0 - at_zero)).astype(BF16)
    own_w = 2.0 * wt[ours, :]
    for own, got, out, at, extra in (
            (own_w, got_a, map_a, 0, firsts),
            (own_w * targ[ours, :], got_b, map_b, 8, jnp.concatenate([firsts[8:16], firsts[0:8]], axis=0))):
        other = got[...].astype(F32)
        direct = jnp.where(low, own, other)
        raw = jnp.where(low, other, own).astype(BF16)
        mirrored = mm(mirror, raw) + mm(pick([(QB * v, at + v) for v in range(4)], rows=128, width=16), firsts_half)
        out[0:128, :] = direct + mm(mirrored.astype(BF16), flip[...])
        out[128:144, :] = jnp.where(sub16 < 4, extra, 0.0) * at_zero
    lines[XB:256, :] = jnp.zeros((256 - XB, NY), BF16)

    def wait_lines(d, carry):
        k = lax.rem(col + d, NCOL)
        for b in range(3):
            line_copy(b, k, k).wait_recv()
        line_rim_copy(k, k).wait_recv()
        return carry

    lax.fori_loop(1, NCOL, wait_lines, 0)
    for b in range(3):
        own_line(b).wait()
    own_rim.wait()

    def worker(b):
        return jnp.where(b // 8 == col // 4, b, 31 - b)

    def spec_at(r, i):
        return spec.at[rows(QB * i, QB), rows(PACK * r, PACK)]

    mine4 = lax.rem(col, 4)

    def half_copy(b):
        return remote(half.at[rows(QB * b, QB), :], spec_at(row, mine4),
                      s2.at[b], r2.at[NROW * row + mine4], plane(worker(b)))

    def half_arrival(r, i):
        return remote(half.at[0:QB, :], spec_at(r, i), s2.at[0], r2.at[NROW * r + i], {"row": r, "col": 4 * vhalf + i})

    own_half = pltpu.make_async_copy(
        half.at[rows(QB * block, QB), :], spec_at(row, mine4), r2.at[NROW * row + mine4])
    is_own = col // 4 == vhalf
    first64 = lanes((128, 128)) < 64

    def along_y(c, carry):
        chunk = lax.rem(c + block // 4 + 1, 4)
        q = rows(128 * chunk, 128)
        q_im = rows(HALF + 128 * chunk, 128)
        re = mm_nt(t1[q, :], lines[...]) + mm(t1rim[q, :], rim_in[...])
        im = mm_nt(t1[q_im, :], lines[...]) + mm(t1rim[q_im, :], rim_in[...])
        re0, re1 = re[:, 0:128], re[:, 128:256]
        im0, im1 = im[:, 0:128], im[:, 128:256]
        half[q, 0:128] = jnp.where(first64, re0, pltpu.roll(im0, 64, 1)).astype(BF16)
        half[q, 128:256] = jnp.where(first64, pltpu.roll(re0, 64, 1), im0).astype(BF16)
        half[q, 256:384] = jnp.where(first64, re1, pltpu.roll(im1, 64, 1)).astype(BF16)
        for m in range(4):
            b = 4 * chunk + m

            @pl.when(worker(b) != me)
            def _():
                half_copy(b).start()

            @pl.when(worker(b) == me)
            def _():
                own_half.start()

        return carry

    lax.fori_loop(0, 4, along_y, 0)

    def wait_half(n, carry):
        r = n // 4
        i = lax.rem(n, 4)
        own = (r == row) & (4 * vhalf + i == col)

        @pl.when(own)
        def _():
            own_half.wait()

        @pl.when(jnp.logical_not(own))
        def _():
            half_arrival(r, i).wait_recv()

        return carry

    lax.fori_loop(0, 16, wait_half, 0)

    lane_w = lanes((16, 2 * NX))
    sub_w = lax.broadcasted_iota(jnp.int32, (16, 2 * NX), 0)
    second_w = lax.rem(lane_w, 128) >= 64
    extra = jnp.zeros((16, 2 * NX), F32)
    for i in range(4):
        tile = spec[QB * i : QB * i + 16, :].astype(F32)
        moved = jnp.concatenate([pltpu.roll(tile[:, 128 * n : 128 * n + 128], 64, 1) for n in range(12)], axis=1)
        extra = jnp.where(jnp.logical_not(second_w) & (sub_w == i), moved[0:1, :], extra)
        spec[QB * i : QB * i + 16, :] = jnp.where(second_w & (sub_w == 0), tile * (1.0 - at_zero), tile).astype(BF16)
    spec[128:144, :] = (extra * at_zero).astype(BF16)

    def along_x(c, carry):
        p = rows(256 * c, 256)
        p_im = rows(NX + 256 * c, 256)
        re = mm(spec[...], t2[:, p])
        im = mm(spec[...], t2[:, p_im])
        factor = map_a[:, p] - map_b[:, p] / jnp.sqrt(re * re + im * im + 1.0)
        grads[:, p] = (factor * re).astype(BF16)
        grads[:, p_im] = (factor * im).astype(BF16)
        return carry

    lax.fori_loop(0, 3, along_x, 0)

    def back_copy(r, i):
        return remote(back.at[r, rows(QB * i, QB), :], coef.at[rows(QB * block, QB), :],
                      s3.at[NROW * r + i], r3.at[block], {"row": r, "col": 4 * vhalf + i})

    def back_arrival(b):
        return remote(back.at[0, 0:QB, :], coef.at[rows(QB * b, QB), :], s3.at[0], r3.at[b], plane(worker(b)))

    own_back = pltpu.make_async_copy(
        back.at[row, rows(QB * mine4, QB), :], coef.at[rows(QB * block, QB), :], r3.at[block])
    lane_b = lanes((16, PACK))
    sub_b = lax.broadcasted_iota(jnp.int32, (16, PACK), 0)
    second_b = (lax.rem(lane_b, 128) >= 64) & (sub_b == 0)

    def back_x(c, carry):
        r = lax.rem(row + 1 + c, NROW)
        got = mm_nt(grads[...], t2[rows(PACK * r, PACK), :])
        back[r] = got[0:128].astype(BF16)
        last = got[128:144]
        moved = jnp.concatenate([pltpu.roll(last[:, 128 * n : 128 * n + 128], 64, 1) for n in range(3)], axis=1)
        for i in range(4):
            tile = got[QB * i : QB * i + 16]
            fixed = tile * (1.0 - at_zero) + moved[i : i + 1, :] * at_zero
            back[r, QB * i : QB * i + 16] = jnp.where(second_b, fixed, tile).astype(BF16)
        for d in range(4):
            i = lax.rem(mine4 + d, 4)
            own = (r == row) & (4 * vhalf + i == col)

            @pl.when(own)
            def _():
                own_back.start()

            @pl.when(jnp.logical_not(own))
            def _():
                back_copy(r, i).start()

        return carry

    lax.fori_loop(0, NROW, back_x, 0)

    def wait_back(b, carry):
        @pl.when(worker(b) == me)
        def _():
            own_back.wait()

        @pl.when(worker(b) != me)
        def _():
            back_arrival(b).wait_recv()

        return carry

    lax.fori_loop(0, 16, wait_back, 0)

    for b in range(3):
        turned = coef[:, 128 * b : 128 * b + 128].T
        flat[64 * b : 64 * b + 64, 0:HALF] = turned[0:64]
        flat[64 * b : 64 * b + 64, HALF:NY] = turned[64:128]

    def tile_copy(k, source):
        return remote(dp_out.at[k], tiles.at[source], s4.at[k], r4.at[source], {"col": k})

    def tile_rim_copy(k, source):
        return remote(rim_out.at[k], rims.at[rows(16 * source, 16), :], s4h.at[k], r4h.at[source], {"col": k})

    own_tile = pltpu.make_async_copy(dp_out.at[col], tiles.at[col], r4.at[col])
    own_tile_rim = pltpu.make_async_copy(rim_out.at[col], rims.at[rows(16 * col, 16), :], r4h.at[col])

    def back_y(c, carry):
        two = lax.rem(c + col // 2 + 1, NCOL // 2)
        cells = mm(flat[...], t1[:, rows(256 * two, 256)]).astype(BF16)
        for m in range(2):
            k = 2 * two + m
            dp_out[k] = cells[:, 128 * m : 128 * m + 128]

            @pl.when(k != col)
            def _():
                tile_copy(k, col).start()

            @pl.when(k == col)
            def _():
                own_tile.start()

        return carry

    lax.fori_loop(0, NCOL // 2, back_y, 0)
    before = pick([(0, YB - 1)])
    after = pick([(1, 0)])
    for k in range(NCOL):
        edge = jnp.zeros((16, XB), F32)
        if k > 0:
            edge = edge + mm_nt(before, dp_out[k - 1])
        if k < NCOL - 1:
            edge = edge + mm_nt(after, dp_out[k + 1])
        rim_out[k] = jnp.concatenate([edge, jnp.zeros((16, 256 - XB), F32)], axis=1).astype(BF16)

        @pl.when(k != col)
        def _():
            tile_rim_copy(k, col).start()

        @pl.when(k == col)
        def _():
            own_tile_rim.start()

    own_tile.wait()
    own_tile_rim.wait()

    def wait_tiles(d, carry):
        k = lax.rem(col + d, NCOL)
        tile_copy(k, k).wait_recv()
        tile_rim_copy(k, k).wait_recv()
        return carry

    lax.fori_loop(1, NCOL, wait_tiles, 0)

    columns[...] = rims[...].astype(F32).T
    place = pick([(16 * v, 0) for v in range(V)] + [(16 * v + 1, YB - 1) for v in range(V)], rows=128)
    of_variable = (lax.broadcasted_iota(jnp.int32, (GROUP, V, YB), 2) // 16
                   == lax.broadcasted_iota(jnp.int32, (GROUP, V, YB), 1))

    def widen(g, carry):
        at = rows(GROUP * g, GROUP)
        cells = jnp.swapaxes(tiles[:, at, :].astype(F32), 0, 1).reshape(V * GROUP, YB)
        edge = jnp.where(of_variable, columns[at, :].reshape(GROUP, 1, YB), 0.0)
        edge = mm(edge.reshape(V * GROUP, YB).astype(BF16), place)
        later = jnp.where(lane128 == YB - 1, edge, pltpu.roll(cells, YB - 1, 1))
        sooner = jnp.where(lane128 == 0, edge, pltpu.roll(cells, 1, 1))
        wide = jnp.concatenate(
            [one.reshape(GROUP, V, YB) for one in (later, cells, sooner, jnp.zeros((V * GROUP, YB), F32))], axis=1)
        shifted[pl.ds(pl.multiple_of(32 + 512 * g, 32), 512), :] = wide.reshape(32 * GROUP, YB).astype(BF16)
        return carry

    lax.fori_loop(0, GROUPS, widen, 0)
    rim_down = remote(shifted.at[32 * XB : 32 * XB + 32], shifted.at[0:32], sy.at[0], ry.at[0], {"row": down})
    rim_up = remote(shifted.at[32:64], shifted.at[32 * XB + 32 : 32 * XB + 64], sy.at[1], ry.at[1], {"row": up})
    rim_down.start()
    rim_up.start()

    def gather(g, total):
        for pair in range(GROUP // 2):
            x = GROUP * g + 2 * pair
            at = pl.multiple_of(32 * x, 32)
            moved = jnp.concatenate([shifted[pl.ds(at, 96), :], shifted[pl.ds(at + 32, 96), :]], axis=1)
            total = total + mm_nt(jnp.concatenate([ft[x], ft[x + 1]], axis=1), moved)
        return total

    total = lax.fori_loop(1, GROUPS - 1, gather, jnp.zeros((C, 96), F32))
    rim_down.wait()
    rim_up.wait()

    @pl.when(row == 0)
    def _():
        shifted[0:32] = jnp.zeros((32, YB), BF16)

    @pl.when(row == NROW - 1)
    def _():
        shifted[32 * XB + 32 : 32 * XB + 64] = jnp.zeros((32, YB), BF16)

    total = gather(0, total)
    total = gather(GROUPS - 1, total)
    total = jnp.concatenate([total, jnp.zeros((C, 128 - 96), F32)], axis=1)
    part[0:C, :] = total
    part[C:128, :] = jnp.zeros((128 - C, 128), F32)

    def sixteen(n):
        return {"dp": n // NROW, "row": lax.rem(n, NROW)}

    def part_copy(n, source):
        return remote(part.at[rows(8 * n, 8)], slots.at[source], sa.at[n], ra.at[source], sixteen(n))

    def col_copy(k, source):
        return remote(mine, slots_col.at[source], sb.at[k], rb.at[source], {"col": k})

    def sum_copy(n, source):
        return remote(total_ref, grad.at[rows(8 * source, 8)], sc.at[n], rc.at[source], sixteen(n))

    def others16(act):
        def one(d, carry):
            act(lax.rem(group16 + d, 16))
            return carry

        lax.fori_loop(1, 16, one, 0)

    def others8(act):
        def one(d, carry):
            act(lax.rem(col + d, NCOL))
            return carry

        lax.fori_loop(1, NCOL, one, 0)

    others16(lambda n: part_copy(n, group16).start())
    slots[group16] = part[rows(8 * group16, 8), :]
    others16(lambda n: part_copy(n, n).wait_recv())
    partial = slots[0]
    for n in range(1, 16):
        partial = partial + slots[n]
    mine[...] = partial
    others8(lambda k: col_copy(k, col).start())
    slots_col[col] = partial
    others8(lambda k: col_copy(k, k).wait_recv())
    partial = slots_col[0]
    for n in range(1, NCOL):
        partial = partial + slots_col[n]
    total_ref[...] = partial
    others16(lambda n: sum_copy(n, group16).start())
    grad[rows(8 * group16, 8), :] = partial
    others16(lambda n: sum_copy(n, n).wait_recv())

    others16(lambda n: part_copy(n, group16).wait_send())
    others16(lambda n: sum_copy(n, group16).wait_send())
    swap_a.wait_send()
    swap_b.wait_send()

    @pl.when(me >= 16)
    def _():
        row_low.wait_send()
        row_high.wait_send()

    def finish_col(k):
        for b in range(3):
            line_copy(b, k, col).wait_send()
        line_rim_copy(k, col).wait_send()
        tile_copy(k, col).wait_send()
        tile_rim_copy(k, col).wait_send()
        col_copy(k, col).wait_send()

    others8(finish_col)

    def finish_half(b, carry):
        @pl.when(worker(b) != me)
        def _():
            half_copy(b).wait_send()

        r = b // 4
        i = lax.rem(b, 4)

        @pl.when(jnp.logical_not((r == row) & (4 * vhalf + i == col)))
        def _():
            back_copy(r, i).wait_send()

        return carry

    lax.fori_loop(0, 16, finish_half, 0)


def main_part(features, weights, target, weight):
    along_y, rim, along_x, flip = spectral_tables()
    vmem = pl.BlockSpec(memory_space=pltpu.VMEM)
    anywhere = pl.BlockSpec(memory_space=pl.ANY)
    dma = pltpu.SemaphoreType.DMA

    def b16(*shape):
        return pltpu.VMEM(shape, BF16)

    def f32(*shape):
        return pltpu.VMEM(shape, F32)

    return pl.pallas_call(
        main_kernel,
        in_specs=[anywhere, vmem] + [anywhere] * 6,
        out_specs=[vmem] * 2,
        out_shape=[
            jax.ShapeDtypeStruct((32 * (XB + 2), YB), BF16),
            jax.ShapeDtypeStruct((128, 128), F32),
        ],
        scratch_shapes=[
            b16(C, XB, YB), b16(XB, C, YB), f32(XB + 2, 72, YB), b16(V, XB, YB), b16(V, XB, YB), b16(V, 16, 256),
            b16(NY, NY), b16(NY, 16 * NCOL), b16(2 * NX, 2 * NX), b16(NX, NX), f32(V * QB, NX), f32(V * QB, NX),
            b16(V * QB, NX), b16(V * QB, NX), b16(128, NX), b16(128, NX), f32(2, 16, NX), f32(16, NX),
            f32(144, NX), f32(144, NX),
            b16(256, NY), b16(16 * NCOL, 256), b16(HALF, PACK), b16(144, 2 * NX), b16(144, 2 * NX),
            b16(NROW, 128, PACK), b16(HALF, PACK), b16(XB, NY), b16(NCOL, XB, YB), b16(NCOL, 16, 256),
            b16(V, XB, YB), b16(V * 16, 256), f32(256, 128),
            f32(128, 128), f32(16, 8, 128), f32(8, 128), f32(NCOL, 8, 128), f32(8, 128),
            dma((GROUPS,)), dma((6,)), dma((2,)), dma((2,)), dma((4,)), dma((3,)),
            dma((3, NCOL)), dma((3, NCOL)), dma((NCOL,)), dma((NCOL,)),
            dma((16,)), dma((16,)), dma((16,)), dma((16,)),
            dma((NCOL,)), dma((NCOL,)), dma((NCOL,)), dma((NCOL,)), dma((2,)), dma((2,)),
            dma((16,)), dma((16,)), dma((NCOL,)), dma((NCOL,)), dma((16,)), dma((16,)),
        ],
        compiler_params=pltpu.CompilerParams(
            collective_id=0, has_side_effects=True, vmem_limit_bytes=VMEM_LIMIT),
        name="main_part",
    )(features, weights, jnp.asarray(along_y), jnp.asarray(rim), jnp.asarray(along_x), jnp.asarray(flip),
      target, weight)


STEP = 96


def fgrad_kernel(shifted, w, out, turn):
    group = pl.program_id(0)

    def pair(n, carry):
        at = pl.multiple_of(32 * (STEP * group + 2 * n), 32)
        moved = jnp.concatenate([shifted[pl.ds(at, 96), :], shifted[pl.ds(at + 32, 96), :]], axis=1)
        got = mm(w[...], moved).astype(BF16)
        turn[2 * n] = got[:, 0:YB]
        turn[2 * n + 1] = got[:, YB : 2 * YB]
        return carry

    lax.fori_loop(0, STEP // 2, pair, 0, unroll=8)

    def turn_back(n, carry):
        at = pl.ds(pl.multiple_of(16 * n, 16), 16)
        out[:, at, :] = jnp.swapaxes(turn[at], 0, 1)
        return carry

    lax.fori_loop(0, STEP // 16, turn_back, 0)


def feature_gradient(shifted, weights):
    return pl.pallas_call(
        fgrad_kernel,
        grid=(XB // STEP,),
        in_specs=[
            pl.BlockSpec((32 * (XB + 2), YB), lambda i: (0, 0)),
            pl.BlockSpec((C, 96), lambda i: (0, 0)),
        ],
        out_specs=pl.BlockSpec((C, STEP, YB), lambda i: (0, i, 0)),
        out_shape=jax.ShapeDtypeStruct((C, XB, YB), BF16),
        scratch_shapes=[pltpu.VMEM((STEP, C, YB), BF16)],
        compiler_params=pltpu.CompilerParams(vmem_limit_bytes=VMEM_LIMIT),
        name="feature_gradient",
    )(shifted, weights)


def per_device(features, kernel, target_amp, spec_weight):
    by_tap = kernel.transpose(2, 3, 0, 1)
    w_forward = jnp.pad(by_tap.reshape(72, C), ((0, 8), (0, 0)))
    w_back = jnp.pad(by_tap[::-1], ((0, 0), (0, 1), (0, 0), (0, 0))).reshape(96, C).T
    shifted, grad = main_part(features.reshape(C, XB, YB), w_forward,
                              target_amp.reshape(V * QB, NX), spec_weight.reshape(V * QB, NX))
    feature_grad = feature_gradient(shifted, w_back).reshape(1, C, XB, YB)
    grad = grad[0:C, 0:96].reshape(C, 3, 4, V)[:, ::-1, 0:3].transpose(3, 0, 1, 2)
    cells = NDP * NX * NY
    return grad / cells, feature_grad


def solution(mesh):
    return jax.shard_map(
        per_device,
        mesh=mesh,
        in_specs=(
            P("dp", None, "row", "col"),
            P(),
            P("dp", None, ("row", "col"), None),
            P(None, ("row", "col"), None),
        ),
        out_specs=(P(), P("dp", None, "row", "col")),
        check_vma=False,
    )
```
